32 devices in a mesh: row: 4 (over y, x), col: 8 (over z, core).
Axes of the slice: x: 2, y: 2, z: 4, core: 2. Of those that a mesh axis runs over, the one named last changes fastest.
Arguments:
- sources: bfloat16 [8192, 1024], P(('row', 'col')), may hold values from -6 to 6
- leaf_in: bfloat16 [32, 256, 256], P(('row', 'col')), may hold values from -0.375 to 0.375
- transfers: bfloat16 [32, 5, 2, 256, 256], P(('row', 'col')), may hold values from -0.25 to 0.25
- leaf_out: bfloat16 [32, 256, 256], P(('row', 'col')), may hold values from -0.375 to 0.375
- tile_mats: bfloat16 [32, 5, 256, 256], P(('row', 'col')), may hold values from -0.375 to 0.375
- tile_list: int32 [32, 5], P(('row', 'col')), may hold values from 0 to 1, as said below
Outputs:
- applied: bfloat16 [8192, 1024], P(('row', 'col'))
The draws below stay inside these ranges and needn't reach their ends.
Inputs may be any that keep to these rules, and one draw needn't show every extreme that they name: tile_list[b, k] is 1 where source block b holds a tile onto the block k - 2 places further along its row of 8 blocks; always 1 for k = 2, always 0 where that block lies outside the row; blocks hold different numbers of tiles.
All inputs are finite; a program needn't handle non-finite values.
Results may differ from the reference program's by a relative error of at most 0.015.
Values may be sent and summed in bfloat16 or wider, within the bound.
A program may use at most 64 MiB of HBM per device.

```python
import jax
import jax.numpy as jnp

RANK = 256
VECS = 1024
TILES = 5
BLOCKS = 32
COL_BLOCKS = 8
LROW = 2
LCOL = 3
LEVELS = 5
N_ROW = 4
N_COL = 8


def draw_tile_list(key, part):
    base = jax.random.fold_in(key, 11)
    first, second = jax.random.split(base)
    level = jax.random.randint(first, (BLOCKS, 1), 1, 5)
    rolled = jax.random.randint(second, (BLOCKS, TILES), 0, 4)
    live = (rolled < level).astype(jnp.int32)
    column = (jnp.arange(BLOCKS, dtype=jnp.int32) % COL_BLOCKS)[:, None]
    offsets = jnp.arange(TILES, dtype=jnp.int32)[None, :] - TILES // 2
    target = column + offsets
    inside = (target >= 0) & (target < COL_BLOCKS)
    live = jnp.where(inside, live, 0)
    live = jnp.where(offsets == 0, 1, live)
    return live.astype(jnp.int32)


def block_scale(rng, extent, cuts, low, top_value):
    loudness, own = 1.0, jax.random.fold_in(rng, 6)
    for position, parts in cuts:
        draws = jnp.exp(jax.random.uniform(jax.random.fold_in(own, position), (parts,), jnp.float32, low / len(cuts), top_value / len(cuts)))
        loudness = loudness * jnp.repeat(draws, extent[position] // parts).reshape([-1 if axis == position else 1 for axis in range(len(extent))])
    return loudness


def noise(stream_key, extent, deviation, reach, pieces=(), held_as=jnp.bfloat16):
    result = jax.random.normal(stream_key, extent, jnp.float32) * deviation
    if len(pieces) > 0:
        result = block_scale(stream_key, extent, pieces, -0.22, 0.18) * result
    return jnp.clip(result, min=-reach, max=reach).astype(held_as)


def setup_inputs(seed: int = 0) -> dict:
    seeds = jax.random.split(jax.random.key(seed), 7)
    return {
        "sources": noise(seeds[0], (BLOCKS * RANK, VECS), 1.0, 6.0, ((0, 32),)),
        "leaf_in": noise(seeds[1], (BLOCKS, RANK, RANK), RANK ** -0.5, 0.375, ((0, 32),)),
        "transfers": noise(seeds[2], (BLOCKS, LEVELS, 2, RANK, RANK), (2 * RANK) ** -0.5, 0.25, ((0, 32),)),
        "leaf_out": noise(seeds[3], (BLOCKS, RANK, RANK), RANK ** -0.5, 0.375, ((0, 32),)),
        "tile_mats": noise(seeds[4], (BLOCKS, TILES, RANK, RANK), RANK ** -0.5, 0.375, ((0, 32),)),
        "tile_list": draw_tile_list(jax.random.fold_in(seeds[6], 71), 0),
    }


def batch_mul(mats, vecs):
    return jnp.einsum("bij,bjv->biv", mats.astype(jnp.float32), vecs.astype(jnp.float32))


def partner_of(coeffs, bit):
    shaped = coeffs.reshape(BLOCKS // (2 ** (bit + 1)), 2, 2 ** bit, RANK, VECS)
    return shaped[:, ::-1].reshape(BLOCKS, RANK, VECS)


def shift_cols(values, offset):
    grid = values.reshape(N_ROW, N_COL, RANK, VECS)
    if offset > 0:
        grid = jnp.pad(grid, ((0, 0), (offset, 0), (0, 0), (0, 0)))[:, :N_COL]
    elif offset < 0:
        grid = jnp.pad(grid, ((0, 0), (0, -offset), (0, 0), (0, 0)))[:, -offset:]
    return grid.reshape(BLOCKS, RANK, VECS)


def reference(sources, leaf_in, transfers, leaf_out, tile_mats, tile_list):
    blocks = sources.reshape(BLOCKS, RANK, VECS)
    coeffs = batch_mul(leaf_in, blocks).astype(jnp.bfloat16)
    for level in range(LEVELS):
        if level < LROW:
            bit = LCOL + level
        else:
            bit = level - LROW
        partner = partner_of(coeffs, bit)
        mixed = batch_mul(transfers[:, level, 0], coeffs) + batch_mul(transfers[:, level, 1], partner)
        coeffs = mixed.astype(jnp.bfloat16)
    far = batch_mul(leaf_out, coeffs)
    live = tile_list.astype(jnp.float32)
    near = jnp.zeros((BLOCKS, RANK, VECS), jnp.float32)
    for k in range(TILES):
        product = batch_mul(tile_mats[:, k], blocks) * live[:, k][:, None, None]
        near = near + shift_cols(product, k - TILES // 2)
    return (far + near).astype(jnp.bfloat16).reshape(BLOCKS * RANK, VECS)
```

```python
import functools

import jax
import jax.numpy as jnp
from jax import lax
from jax.experimental import pallas as pl
from jax.experimental.pallas import tpu as pltpu
from jax.sharding import PartitionSpec as P

MESH = pl.DeviceIdType.MESH
CHUNKS = 4
VMEM_BYTES = 60 * 1024 * 1024


def dot(mats, vectors):
    return jnp.dot(mats, vectors, preferred_element_type=jnp.float32)


def level_plan(rows, cols):
    high = [("row", 1 << b) for b in range(rows.bit_length() - 1)]
    low = [("col", 1 << b) for b in range(cols.bit_length() - 1)]
    return high + low


def task_order(plan, chunks):
    when = {}
    for l, (axis, apart) in enumerate(plan):
        hop = 1.0 if axis == "row" else (0.25 if apart == 1 else 0.65 * apart)
        for c in range(chunks):
            ready = when[l - 1, c] if l else 0.1 * c
            free = when[l, c - 1] if c else 0.0
            when[l, c] = max(ready, free) + hop
    return sorted(when, key=lambda task: (when[task], task))


def kernel(plan, chunks, src, w_in, trans, w_out, tiles, live, out,
           s_own, s_peer, coef, got, win_v, tr_v, wout_v, tl_v, tm_v, tp_own, tp_peer,
           near_out, near_in, acc, out_v,
           src_sem, load_sem, lsend, lrecv, ssend, srecv, tsend, trecv, nsend, nrecv, osem):
    row, col = lax.axis_index("row"), lax.axis_index("col")
    cols = lax.axis_size("col")
    levels = len(plan)
    width = s_own.shape[-1]

    def load(source, target, sem):
        copy = pltpu.make_async_copy(source, target, sem)
        copy.start()
        return copy

    src_loads = []
    for c in range(chunks):
        src_loads.append(
            load(src.at[:, pl.ds(c * width, width)], s_own.at[c], src_sem.at[c])
        )
        if c == 0:
            win_load = load(w_in.at[0], win_v, load_sem.at[0])
            tile_load = load(tiles.at[0], tl_v, load_sem.at[1])
    trans_load = load(trans.at[0], tr_v, load_sem.at[2])
    wout_load = load(w_out.at[0], wout_v, load_sem.at[3])

    def partner(level):
        axis, apart = plan[level]
        at = row if axis == "row" else col
        other = at + apart * (1 - 2 * ((at // apart) % 2))
        return (other, col) if axis == "row" else (row, other)

    odd = col % 2
    step = 2 - 4 * odd
    peer = (row, col + 1 - 2 * odd)
    ahead, behind = col + step, col - step
    has_ahead = jnp.logical_and(ahead >= 0, ahead < cols)
    has_behind = jnp.logical_and(behind >= 0, behind < cols)

    barrier = pltpu.get_barrier_semaphore()
    for level in range(levels):
        pl.semaphore_signal(barrier, inc=1, device_id=partner(level), device_id_type=MESH)

    @pl.when(has_ahead)
    def _():
        pl.semaphore_signal(barrier, inc=1, device_id=(row, ahead), device_id_type=MESH)

    @pl.when(has_behind)
    def _():
        pl.semaphore_signal(barrier, inc=1, device_id=(row, behind), device_id_type=MESH)

    pl.semaphore_wait(
        barrier, levels + has_ahead.astype(jnp.int32) + has_behind.astype(jnp.int32)
    )

    @pl.when(jnp.logical_not(has_behind))
    def _():
        near_in[0] = jnp.zeros_like(near_in[0])

    @pl.when(jnp.logical_not(has_ahead))
    def _():
        near_in[1] = jnp.zeros_like(near_in[1])

    def level_copy(level, c):
        return pltpu.make_async_remote_copy(
            src_ref=coef.at[level, c], dst_ref=got.at[level, c],
            send_sem=lsend.at[level, c], recv_sem=lrecv.at[level, c],
            device_id=partner(level), device_id_type=MESH)

    def source_copy(c):
        return pltpu.make_async_remote_copy(
            src_ref=s_own.at[c], dst_ref=s_peer.at[c],
            send_sem=ssend.at[c], recv_sem=srecv.at[c],
            device_id=peer, device_id_type=MESH)

    tile_copy = pltpu.make_async_remote_copy(
        src_ref=tp_own, dst_ref=tp_peer, send_sem=tsend.at[0], recv_sem=trecv.at[0],
        device_id=peer, device_id_type=MESH)

    def near_copy(way, c):
        to = ahead if way == 0 else behind
        return pltpu.make_async_remote_copy(
            src_ref=near_out.at[way, c], dst_ref=near_in.at[way, c],
            send_sem=nsend.at[way, c], recv_sem=nrecv.at[way, c],
            device_id=(row, to), device_id_type=MESH)

    for c in range(chunks):
        src_loads[c].wait()
        source_copy(c).start()
        if c == 0:
            win_load.wait()
        coef[0, c] = dot(win_v[...], s_own[c]).astype(coef.dtype)
        level_copy(0, c).start()
        if c == 0:
            tile_load.wait()
            for k in range(tl_v.shape[0]):
                kept = tl_v[k].astype(jnp.float32) * live[0, k].astype(jnp.float32)
                kept = kept.astype(tm_v.dtype)
                tm_v[k] = kept
                if k in (1, 3):
                    tp_own[k // 2] = kept
            tile_copy.start()

        @pl.when(has_behind)
        def _():
            near_out[1, c] = dot(tm_v[4 * odd], s_own[c]).astype(near_out.dtype)
            near_copy(1, c).start()

    tile_copy.wait_recv()
    for c in range(chunks):
        source_copy(c).wait_recv()

        @pl.when(has_ahead)
        def _():
            total = dot(tm_v[4 - 4 * odd], s_own[c]) + dot(tp_peer[1 - odd], s_peer[c])
            near_out[0, c] = total.astype(near_out.dtype)
            near_copy(0, c).start()

    for c in range(chunks):
        acc[c] = dot(tm_v[2], s_own[c]) + dot(tp_peer[odd], s_peer[c])

    trans_load.wait()
    wout_load.wait()
    stores = []
    for level, c in task_order(plan, chunks):
        last = level == levels - 1
        if last:
            @pl.when(has_behind)
            def _():
                near_copy(0, c).wait_recv()

            @pl.when(has_ahead)
            def _():
                near_copy(1, c).wait_recv()

            acc[c] += near_in[0, c].astype(jnp.float32) + near_in[1, c].astype(jnp.float32)

        level_copy(level, c).wait_recv()
        mixed = dot(tr_v[level, 0], coef[level, c]) + dot(tr_v[level, 1], got[level, c])
        mixed = mixed.astype(coef.dtype)
        if last:
            out_v[c] = (dot(wout_v[...], mixed) + acc[c]).astype(out_v.dtype)
            stores.append(
                load(out_v.at[c], out.at[:, pl.ds(c * width, width)], osem.at[c])
            )
        else:
            coef[level + 1, c] = mixed
            level_copy(level + 1, c).start()

    tile_copy.wait_send()
    for c in range(chunks):
        source_copy(c).wait_send()
        for level in range(levels):
            level_copy(level, c).wait_send()

        @pl.when(has_ahead)
        def _():
            near_copy(0, c).wait_send()

        @pl.when(has_behind)
        def _():
            near_copy(1, c).wait_send()

    for store in stores:
        store.wait()


def shards(sources, leaf_in, transfers, leaf_out, tile_mats, tile_list):
    plan = level_plan(lax.axis_size("row"), lax.axis_size("col"))
    levels = len(plan)
    rank, vecs = sources.shape
    count = tile_mats.shape[1]
    chunks = CHUNKS
    width = vecs // chunks
    half = jnp.bfloat16
    block = (chunks, rank, width)
    dma = pltpu.SemaphoreType.DMA
    anywhere = pl.BlockSpec(memory_space=pl.ANY)
    flops = 2 * rank * rank * vecs * (2 * levels + count + 4)
    return pl.pallas_call(
        functools.partial(kernel, plan, chunks),
        out_shape=jax.ShapeDtypeStruct((rank, vecs), half),
        in_specs=[anywhere] * 5 + [pl.BlockSpec(memory_space=pltpu.SMEM)],
        out_specs=anywhere,
        scratch_shapes=[
            pltpu.VMEM(block, half),
            pltpu.VMEM(block, half),
            pltpu.VMEM((levels,) + block, half),
            pltpu.VMEM((levels,) + block, half),
            pltpu.VMEM((rank, rank), half),
            pltpu.VMEM((levels, 2, rank, rank), half),
            pltpu.VMEM((rank, rank), half),
            pltpu.VMEM((count, rank, rank), half),
            pltpu.VMEM((count, rank, rank), half),
            pltpu.VMEM((2, rank, rank), half),
            pltpu.VMEM((2, rank, rank), half),
            pltpu.VMEM((2,) + block, half),
            pltpu.VMEM((2,) + block, half),
            pltpu.VMEM(block, jnp.float32),
            pltpu.VMEM(block, half),
            dma((chunks,)),
            dma((4,)),
            dma((levels, chunks)),
            dma((levels, chunks)),
            dma((chunks,)),
            dma((chunks,)),
            dma((1,)),
            dma((1,)),
            dma((2, chunks)),
            dma((2, chunks)),
            dma((chunks,)),
        ],
        compiler_params=pltpu.CompilerParams(
            collective_id=0, has_side_effects=True, vmem_limit_bytes=VMEM_BYTES
        ),
        cost_estimate=pl.CostEstimate(
            flops=flops, bytes_accessed=8 * 1024 * 1024, transcendentals=0
        ),
    )(sources, leaf_in, transfers, leaf_out, tile_mats, tile_list)


def solution(mesh):
    return jax.shard_map(
        shards,
        mesh=mesh,
        in_specs=(
            P(("row", "col"), None),
            P(("row", "col"), None, None),
            P(("row", "col"), None, None, None, None),
            P(("row", "col"), None, None),
            P(("row", "col"), None, None, None),
            P(("row", "col"), None),
        ),
        out_specs=P(("row", "col"), None),
        check_vma=False,
    )
```
